32 devices in a mesh: px: 8 (over z, core), py: 4 (over y, x).
Axes of the slice: x: 2, y: 2, z: 4, core: 2. Of those that a mesh axis runs over, the one named last changes fastest.
Arguments:
- phase: float32 [384, 384, 384], P('px', 'py'), may hold values from -2.5 to 2.5
- material: float32 [384, 384, 384], P('px', 'py'), may hold values from 0.5 to 2
- source: float32 [384, 384, 384], P('px', 'py'), may hold values from -6 to 6
Outputs:
- phase_next: float32 [384, 384, 384], P('px', 'py')
- concentration: float32 [384, 384, 384], P('px', 'py')
The draws below stay inside these ranges and needn't reach their ends.
All inputs are finite; a program needn't handle non-finite values.
Results may differ from the reference program's by a relative error of at most 0.00015.
Values sent between devices are 32-bit elements; how exact they have to be, the bound alone decides.
A program may use at most 256 MiB of HBM per device.

```python
import math
import jax
import jax.numpy as jnp

NX = 384
NY = 384
NZ = 384
ITERS = 2


def draw_phase(key, part):
    angles = jax.random.uniform(jax.random.fold_in(key, 3), (3,), jnp.float32, -jnp.pi, jnp.pi)
    x_wave = jnp.cos(2.0 * jnp.pi * jnp.arange(NX).astype(jnp.float32) / NX + angles[0])
    y_wave = jnp.cos(2.0 * jnp.pi * jnp.arange(NY).astype(jnp.float32) / NY + angles[1])
    rough = jnp.clip(jax.random.normal(jax.random.fold_in(key, 5), (NX, NY, NZ), jnp.float32), -4.0, 4.0)
    smooth = x_wave[:, None, None] * y_wave[None, :, None]
    return 0.57735 * rough + 0.15 * smooth


def draw_source(key, part):
    ramp = 0.5 + jnp.arange(NX).astype(jnp.float32) / NX
    base = jnp.clip(jax.random.normal(key, (NX, NY, NZ), jnp.float32), -4.0, 4.0)
    return base * ramp[:, None, None]


def block_levels(rng, dims, shards, least, largest):
    def one(dim, blocks):
        steps = jax.random.uniform(jax.random.fold_in(jax.random.fold_in(rng, 6), dim), (blocks,), jnp.float32, least / len(shards), largest / len(shards))
        return jnp.repeat(jnp.exp(steps), dims[dim] // blocks).reshape((-1,) + (1,) * (len(dims) - dim - 1))

    loudness = one(*shards[0])
    for cut in shards[1:]:
        loudness = loudness * one(*cut)
    return loudness


def setup_inputs(seed: int = 0) -> dict:
    seeds = jax.random.split(jax.random.key(seed), 4)
    return {
        "phase": draw_phase(jax.random.fold_in(seeds[3], 71), 0),
        "material": jnp.clip(jnp.exp(math.log(2.0) - 1.3862944 * jax.random.uniform(seeds[1], (NX, NY, NZ), jnp.float32) ** block_levels(seeds[1], (NX, NY, NZ), ((0, 8), (1, 4)), -0.2, 0.2)), 0.5, 2.0),
        "source": draw_source(jax.random.fold_in(seeds[3], 71), 0),
    }


DT = 250000.0
KAPPA = 1.0
STAB = 1.0
FLOOR = 0.1
SHARP = 6.0
LEFT_VALUE = 1.0


def symbol(length):
    index = jnp.arange(length).astype(jnp.float32)
    return (2.0 * jnp.sin(jnp.pi * index / length)) ** 2


def filters(k_square):
    denom = 1.0 / (1.0 + DT * (KAPPA + STAB) * k_square * k_square)
    return (1.0 + DT * STAB * k_square * k_square) * denom, -DT * k_square * denom


def reference(phase, material, source):
    nonlin = phase * phase * phase - phase
    k_square = symbol(NX)[:, None, None] + symbol(NY)[None, :, None] + symbol(NZ)[None, None, :]
    damp, push = filters(k_square)
    mixed = damp * jnp.fft.fftn(phase) + push * jnp.fft.fftn(nonlin)
    phase_next = jnp.real(jnp.fft.ifftn(mixed)).astype(phase.dtype)
    conduct = material * (FLOOR + (1.0 - FLOOR) * jax.nn.sigmoid(SHARP * phase_next))
    x_pos = jnp.arange(NX)[:, None, None]
    low_edge = x_pos == 0
    high_edge = x_pos == NX - 1
    face_xl = jnp.where(low_edge, conduct, 0.5 * (conduct + jnp.roll(conduct, 1, 0)))
    face_xh = jnp.where(high_edge, conduct, 0.5 * (conduct + jnp.roll(conduct, -1, 0)))
    face_yl = 0.5 * (conduct + jnp.roll(conduct, 1, 1))
    face_yh = 0.5 * (conduct + jnp.roll(conduct, -1, 1))
    face_zl = 0.5 * (conduct + jnp.roll(conduct, 1, 2))
    face_zh = 0.5 * (conduct + jnp.roll(conduct, -1, 2))
    diag = face_xl + face_xh + face_yl + face_yh + face_zl + face_zh
    weight_xl = jnp.where(low_edge, 0.0, face_xl)
    weight_xh = jnp.where(high_edge, 0.0, face_xh)

    def operate(field):
        out = diag * field - weight_xl * jnp.roll(field, 1, 0) - weight_xh * jnp.roll(field, -1, 0)
        out = out - face_yl * jnp.roll(field, 1, 1) - face_yh * jnp.roll(field, -1, 1)
        return out - face_zl * jnp.roll(field, 1, 2) - face_zh * jnp.roll(field, -1, 2)

    rhs = source + jnp.where(low_edge, conduct * LEFT_VALUE, 0.0)
    concentration = jnp.zeros_like(rhs)
    residual, direction = rhs, rhs
    norm_now = jnp.sum(residual * residual)
    for step in range(ITERS):
        image = operate(direction)
        alpha = norm_now / jnp.sum(direction * image)
        concentration = concentration + alpha * direction
        residual = residual - alpha * image
        norm_next = jnp.sum(residual * residual)
        direction = residual + (norm_next / norm_now) * direction
        norm_now = norm_next
    return phase_next, concentration
```

```python
import jax
import jax.numpy as jnp
import numpy as np
from jax import lax
from jax.sharding import PartitionSpec as P

DT = 250000.0
KAPPA = 1.0
STAB = 1.0
FLOOR = 0.1
SHARP = 6.0
LEFT_VALUE = 1.0
HIGH = lax.Precision.HIGH


def halos(value, axis, dim):
    peers, length = (lax.axis_size(axis), value.shape[dim])
    up = [(i, (i + 1) % peers) for i in range(peers)]
    down = [(j, i) for i, j in up]
    before = lax.ppermute(lax.slice_in_dim(value, length - 1, length, axis=dim), axis, up)
    after = lax.ppermute(lax.slice_in_dim(value, 0, 1, axis=dim), axis, down)
    return before, after


def neighbours(value):
    before_x, after_x = halos(value, "px", 0)
    before_y, after_y = halos(value, "py", 1)
    return (
        jnp.concatenate([before_x, value[:-1]], 0),
        jnp.concatenate([value[1:], after_x], 0),
        jnp.concatenate([before_y, value[:, :-1]], 1),
        jnp.concatenate([value[:, 1:], after_y], 1),
        jnp.roll(value, 1, 2),
        jnp.roll(value, -1, 2),
    )


def angles(length, rows, cols):
    product = np.arange(rows)[:, None] * np.arange(cols)[None, :] % length
    angle = 2.0 * np.pi / length * product
    return np.cos(angle), np.sin(angle)


def complex_table(length, sign):
    cos_t, sin_t = angles(length, length, length)
    real = np.stack([cos_t, sign * sin_t], -1)
    imag = np.stack([-sign * sin_t, cos_t], -1)
    return np.stack([real, imag], 1).astype(np.float32)


def symbol(length, count):
    return ((2.0 * np.sin(np.pi * np.arange(count) / length)) ** 2).astype(np.float32)


def exchange(value, axis):
    return lax.all_to_all(value, axis, split_axis=0, concat_axis=0, tiled=True)


def body(phase, material, source):
    lx, ly, lz = phase.shape
    n_px = lax.axis_size("px")
    n_py = lax.axis_size("py")
    ix = lax.axis_index("px")
    iy = lax.axis_index("py")
    full_x = lx * n_px
    full_y = ly * n_py
    total = full_x * full_y * lz
    half = lz // 2 + 1
    kz_loc = -(-half // n_py)
    kz_all = kz_loc * n_py
    ky_loc = full_y // n_px
    cos_z, sin_z = angles(lz, kz_all, lz)
    rows = np.arange(kz_all)
    held = (rows < half).astype(np.float64)[:, None]
    twice = np.where((rows == 0) | (2 * rows == lz), 1.0, 2.0)[:, None] * held / total
    z_fwd = np.stack([cos_z * held, -sin_z * held]).reshape(2, n_py, kz_loc, lz).astype(np.float32)
    z_inv = np.stack([cos_z * twice, -sin_z * twice]).reshape(2, n_py, kz_loc, lz).astype(np.float32)

    fields = jnp.stack([phase, phase * phase * phase - phase])
    spectra = jnp.einsum("fxyz,cpkz->pycfxk", fields, z_fwd, precision=HIGH)
    spectra = exchange(spectra.reshape(n_py, ly, 2, 2, lx * kz_loc), "py")
    spectra = spectra.reshape(full_y, 2, 2, lx * kz_loc)
    spectra = jnp.einsum("qdyc,ycfm->qdfm", complex_table(full_y, 1.0), spectra, precision=HIGH)
    spectra = spectra.reshape(n_px, ky_loc, 2, 2, lx, kz_loc).transpose(0, 4, 2, 3, 1, 5)
    spectra = exchange(spectra.reshape(n_px, lx, 2, 2, ky_loc * kz_loc), "px")
    spectra = spectra.reshape(full_x, 2, 2, ky_loc * kz_loc)
    spectra = jnp.einsum("pdxc,xcfm->fpdm", complex_table(full_x, 1.0), spectra, precision=HIGH)

    y_part = lax.dynamic_slice_in_dim(jnp.asarray(symbol(full_y, full_y)), ix * ky_loc, ky_loc)
    z_part = lax.dynamic_slice_in_dim(jnp.asarray(symbol(lz, kz_all)), iy * kz_loc, kz_loc)
    plane = (y_part[:, None] + z_part[None, :]).reshape(-1)
    k_square = symbol(full_x, full_x)[:, None, None] + plane[None, None, :]
    denom = 1.0 / (1.0 + DT * (KAPPA + STAB) * k_square * k_square)
    damp = (1.0 + DT * STAB * k_square * k_square) * denom
    push = -DT * k_square * denom
    mixed = damp * spectra[0] + push * spectra[1]

    mixed = jnp.einsum("xdpc,pcm->xdm", complex_table(full_x, -1.0), mixed, precision=HIGH)
    mixed = exchange(mixed.reshape(n_px, lx, 2, ky_loc * kz_loc), "px")
    mixed = mixed.reshape(n_px, lx, 2, ky_loc, kz_loc).transpose(0, 3, 2, 1, 4)
    mixed = mixed.reshape(full_y, 2, lx * kz_loc)
    mixed = jnp.einsum("ydqc,qcm->ydm", complex_table(full_y, -1.0), mixed, precision=HIGH)
    mixed = exchange(mixed.reshape(n_py, ly, 2, lx * kz_loc), "py")
    mixed = mixed.reshape(n_py, ly, 2, lx, kz_loc)
    phase_next = jnp.einsum("pycxk,cpkz->xyz", mixed, z_inv, precision=HIGH)

    conduct = material * (FLOOR + (1.0 - FLOOR) * jax.nn.sigmoid(SHARP * phase_next))
    near = neighbours(conduct)
    x_pos = ix * lx + lax.broadcasted_iota(jnp.int32, (lx, 1, 1), 0)
    low_edge = x_pos == 0
    high_edge = x_pos == full_x - 1
    face_xl = jnp.where(low_edge, conduct, 0.5 * (conduct + near[0]))
    face_xh = jnp.where(high_edge, conduct, 0.5 * (conduct + near[1]))
    face_yl, face_yh, face_zl, face_zh = [0.5 * (conduct + other) for other in near[2:]]
    diag = face_xl + face_xh + face_yl + face_yh + face_zl + face_zh
    weight_xl = jnp.where(low_edge, 0.0, face_xl)
    weight_xh = jnp.where(high_edge, 0.0, face_xh)

    def operate(field):
        xl, xh, yl, yh, zl, zh = neighbours(field)
        out = diag * field - weight_xl * xl - weight_xh * xh
        out = out - face_yl * yl - face_yh * yh
        return out - face_zl * zl - face_zh * zh

    def sums(*pairs):
        return lax.psum(jnp.stack([jnp.sum(a * b) for a, b in pairs]), ("px", "py"))

    rhs = source + jnp.where(low_edge, conduct * LEFT_VALUE, 0.0)
    image = operate(rhs)
    norm_now, curve = sums((rhs, rhs), (rhs, image))
    alpha = norm_now / curve
    residual = rhs - alpha * image
    image_r = operate(residual)
    norm_next, curve_r, cross = sums((residual, residual), (residual, image_r), (residual, image))
    beta = norm_next / norm_now
    alpha_2 = norm_next / (curve_r + 2.0 * beta * cross + beta * beta * curve)
    concentration = (alpha + alpha_2 * beta) * rhs + alpha_2 * residual
    return (phase_next, concentration)


def solution(mesh):
    return jax.shard_map(
        body,
        mesh=mesh,
        in_specs=(P("px", "py", None), P("px", "py", None), P("px", "py", None)),
        out_specs=(P("px", "py", None), P("px", "py", None)),
        check_vma=False,
    )
```
